32 devices in a mesh: dp: 16 (over z, y, x), tensor: 2 (over core).
Axes of the slice: x: 2, y: 2, z: 4, core: 2. Of those that a mesh axis runs over, the one named last changes fastest.
Arguments:
- tokens: bfloat16 [16384, 768], P('dp'), may hold values from -6 to 6
- seq_lengths: int32 [32, 4], P('dp'), may hold values from 0 to 512, as said below
- prev_logits: bfloat16 [32, 12, 512, 512], P('dp', 'tensor'), may hold values from -6 to 6
- query_weight: bfloat16 [768, 768], P(None, 'tensor'), may hold values from -0.21875 to 0.21875
- query_bias: float32 [768], P('tensor'), may hold values from -3 to 3
- key_weight: bfloat16 [768, 768], P(None, 'tensor'), may hold values from -0.21875 to 0.21875
- value_weight: bfloat16 [768, 768], P(None, 'tensor'), may hold values from -0.21875 to 0.21875
- value_bias: float32 [768], P('tensor'), may hold values from -3 to 3
- out_weight: bfloat16 [768, 768], P('tensor'), may hold values from -1.75 to 1.75
- out_bias: float32 [768], replicated, may hold values from -3 to 3
- first_gain: float32 [768], replicated, may hold values from 0.5 to 1.5
- first_shift: float32 [768], replicated, may hold values from -3 to 3
- up_weight: bfloat16 [768, 3072], P(None, 'tensor'), may hold values from -0.21875 to 0.21875
- up_bias: float32 [3072], P('tensor'), may hold values from -3 to 3
- down_weight: bfloat16 [3072, 768], P('tensor'), may hold values from -0.109375 to 0.109375
- down_bias: float32 [768], replicated, may hold values from -3 to 3
- second_gain: float32 [768], replicated, may hold values from 0.5 to 1.5
- second_shift: float32 [768], replicated, may hold values from -3 to 3
- out_cotangent: bfloat16 [16384, 768], P(('dp', 'tensor')), may hold values from -6 to 6
Outputs:
- layer_output: bfloat16 [16384, 768], P(('dp', 'tensor'))
- raw_logits: bfloat16 [32, 12, 512, 512], P('dp', 'tensor')
- token_grad: float32 [16384, 768], P(('dp', 'tensor'))
- prev_grad: bfloat16 [32, 12, 512, 512], P('dp', 'tensor')
- query_weight_grad: float32 [768, 768], P(None, 'tensor')
- query_bias_grad: float32 [768], P('tensor')
- key_weight_grad: float32 [768, 768], P(None, 'tensor')
- value_weight_grad: float32 [768, 768], P(None, 'tensor')
- value_bias_grad: float32 [768], P('tensor')
- out_weight_grad: float32 [768, 768], P('tensor')
- out_bias_grad: float32 [768], replicated
- first_gain_grad: float32 [768], replicated
- first_shift_grad: float32 [768], replicated
- up_weight_grad: float32 [768, 3072], P(None, 'tensor')
- up_bias_grad: float32 [3072], P('tensor')
- down_weight_grad: float32 [3072, 768], P('tensor')
- down_bias_grad: float32 [768], replicated
- second_gain_grad: float32 [768], replicated
- second_shift_grad: float32 [768], replicated
The draws below stay inside these ranges and needn't reach their ends.
Inputs may be any that keep to these rules, and one draw needn't show every extreme that they name: `seq_lengths`: each row lists, in order, the lengths of the at most 4 sequences packed into one block of 512 tokens; a sequence of length n occupies 128 * ceil(n / 128) positions, the positions beyond n being padding; the occupied positions of a row add up to exactly 512; unused entries are 0 and follow the used ones; some row holds a single sequence of 512 tokens.
All inputs are finite; a program needn't handle non-finite values.
Results may differ from the reference program's by a relative error of at most 0.015.
Values may be sent and summed in bfloat16 or wider, within the bound.
No kernel may reach another device: no remote copies, remote signals or barrier semaphores. Data moves between devices by JAX's collectives and lax.ppermute only.
A program may use at most 128 MiB of HBM per device.

```python
import math
import jax
import jax.numpy as jnp
import numpy as np
from jax import lax

D = 768
HEADS = 12
HEAD_DIM = 64
FF = 3072
PACK = 512
SLOTS = 4
UNIT = 128
BLOCKS = 32
TOKENS = 16384


LAYOUTS = np.array([[4, 0, 0, 0], [3, 1, 0, 0], [1, 3, 0, 0], [2, 2, 0, 0], [2, 1, 1, 0], [1, 2, 1, 0], [1, 1, 2, 0], [1, 1, 1, 1]], dtype=np.int32)


def draw_seq_lengths(key, part):
    key = jax.random.fold_in(key, 7)
    pick_key, size_key, full_key = jax.random.split(key, 3)
    table = jnp.asarray(LAYOUTS)
    picks = jax.random.randint(pick_key, (BLOCKS,), 0, 8)
    chosen = jax.random.randint(full_key, (), 0, BLOCKS)
    block_ids = jnp.arange(BLOCKS)
    picks = jnp.where(block_ids == chosen, 0, picks)
    units = table[picks]
    extra = jax.random.randint(size_key, (BLOCKS, SLOTS), 1, UNIT + 1)
    lengths = jnp.where(units > 0, (units - 1) * UNIT + extra, 0)
    first = (block_ids == chosen)[:, None] & (jnp.arange(SLOTS) == 0)[None, :]
    return jnp.where(first, PACK, lengths).astype(jnp.int32)


def shard_levels(key, extent, shards, smallest, largest):
    level = 1.0
    for position, blocks in shards:
        heights = jax.random.uniform(jax.random.fold_in(jax.random.fold_in(key, 6), position), (blocks,), jnp.float32, smallest / len(shards), largest / len(shards))
        level = level * jnp.repeat(jnp.exp(heights), extent[position] // blocks).reshape((-1,) + (1,) * (len(extent) - 1 - position))
    return level


def normal_values(own_key, dims, scale, most, cuts=(), held_as=jnp.bfloat16):
    factor_of = shard_levels(own_key, dims, cuts, -0.22, 0.18) if cuts else 1.0
    values = jax.random.normal(own_key, dims, jnp.float32) * scale * factor_of
    return jnp.minimum(jnp.maximum(values, -most), most).astype(held_as)


def setup_inputs(seed: int = 0) -> dict:
    key_list = jax.random.split(jax.random.key(seed), 20)
    tokens = normal_values(key_list[0], (TOKENS, D), 1.0, 6.0, ((0, 16),))
    seq_lengths = draw_seq_lengths(jax.random.fold_in(key_list[19], 71), 0)
    prev_logits = normal_values(key_list[2], (BLOCKS, HEADS, PACK, PACK), 1.0, 6.0, ((0, 16), (1, 2)))
    query_weight = normal_values(key_list[3], (D, D), D ** -0.5, 0.21875, ((1, 2),))
    query_bias = normal_values(key_list[4], (D,), 0.5, 3.0, ((0, 2),), jnp.float32)
    key_weight = normal_values(key_list[5], (D, D), D ** -0.5, 0.21875, ((1, 2),))
    value_weight = normal_values(key_list[6], (D, D), D ** -0.5, 0.21875, ((1, 2),))
    value_bias = normal_values(key_list[7], (D,), 0.5, 3.0, ((0, 2),), jnp.float32)
    out_weight = normal_values(key_list[8], (D, D), (max(D // 64, 8)) ** -0.5, 1.75, ((0, 2),))
    out_bias = normal_values(key_list[9], (D,), 0.5, 3.0, (), jnp.float32)
    first_gain = jnp.clip(1.0 + 0.1 * jax.random.normal(key_list[10], (D,), jnp.float32), 0.5, 1.5)
    first_shift = normal_values(key_list[11], (D,), 0.5, 3.0, (), jnp.float32)
    up_weight = normal_values(key_list[12], (D, FF), D ** -0.5, 0.21875, ((1, 2),))
    up_bias = normal_values(key_list[13], (FF,), 0.5, 3.0, ((0, 2),), jnp.float32)
    down_weight = normal_values(key_list[14], (FF, D), FF ** -0.5, 0.109375, ((0, 2),))
    down_bias = normal_values(key_list[15], (D,), 0.5, 3.0, (), jnp.float32)
    second_gain = jnp.clip(1.0 + 0.1 * jax.random.normal(key_list[16], (D,), jnp.float32), 0.5, 1.5)
    second_shift = normal_values(key_list[17], (D,), 0.5, 3.0, (), jnp.float32)
    out_cotangent = normal_values(key_list[18], (TOKENS, D), 1.0, 6.0, ((0, 32),))
    return {"tokens": tokens, "seq_lengths": seq_lengths, "prev_logits": prev_logits, "query_weight": query_weight, "query_bias": query_bias, "key_weight": key_weight, "value_weight": value_weight, "value_bias": value_bias, "out_weight": out_weight, "out_bias": out_bias, "first_gain": first_gain, "first_shift": first_shift, "up_weight": up_weight, "up_bias": up_bias, "down_weight": down_weight, "down_bias": down_bias, "second_gain": second_gain, "second_shift": second_shift, "out_cotangent": out_cotangent}


@jax.custom_vjp
def low(v):
    return lax.optimization_barrier(v.astype(jnp.bfloat16)).astype(jnp.float32)

@jax.custom_vjp
def low_back(v):
    return v

def low_keep(v):
    return (low(v), None)

def low_pass(kept, grad):
    return (grad,)

def back_keep(v):
    return (v, None)

def back_low(kept, grad):
    return (low(grad),)
low.defvjp(low_keep, low_pass)
low_back.defvjp(back_keep, back_low)
HIGHEST = lax.Precision.HIGHEST

def layout(lengths):
    padded = (lengths + UNIT - 1) // UNIT * UNIT
    finish = jnp.cumsum(padded)
    starts = finish - padded
    places = jnp.arange(PACK, dtype=jnp.int32)
    member = (places[:, None] >= starts[None, :]) & (places[:, None] < finish[None, :])
    slot_ids = jnp.arange(lengths.shape[0], dtype=jnp.int32)
    segment = lax.optimization_barrier(jnp.sum(jnp.where(member, slot_ids[None, :], 0), axis=1))
    inside = jnp.any(member & (places[:, None] - starts[None, :] < lengths[None, :]), axis=1)
    return (segment[:, None] == segment[None, :]) & inside[None, :]

def product(left, right):
    return jnp.dot(left, right, precision=HIGHEST)

def layer_norm(values, gain, shift):
    center = values - lax.optimization_barrier(jnp.mean(values, axis=-1, keepdims=True))
    spread = lax.optimization_barrier(jnp.mean(center * center, axis=-1, keepdims=True))
    return center * lax.rsqrt(spread + 1e-05) * gain + shift

def reference(tokens, seq_lengths, prev_logits, query_weight, query_bias, key_weight, value_weight, value_bias, out_weight, out_bias, first_gain, first_shift, up_weight, up_bias, down_weight, down_bias, second_gain, second_shift, out_cotangent):
    pair_masks = lax.map(layout, seq_lengths)
    score_scale = 1.0 / math.sqrt(HEAD_DIM)

    def attend(pieces):
        query_block, key_block, value_block, prev_block, mask_block = pieces
        scores = jnp.einsum('qhd,khd->hqk', query_block, key_block, precision=HIGHEST) * score_scale + prev_block
        scores = low_back(scores)
        masked = jnp.where(mask_block[None], scores, -1000000000.0)
        row_top = lax.optimization_barrier(jnp.max(masked, axis=-1, keepdims=True))
        powers = jnp.exp(masked - row_top)
        probs = powers / lax.optimization_barrier(jnp.sum(powers, axis=-1, keepdims=True))
        mixed = jnp.einsum('hqk,khd->qhd', low(probs), value_block, precision=HIGHEST)
        return (mixed, scores)

    def forward(token_vals, prev_vals, query_weight, query_bias, key_weight, value_weight, value_bias, out_weight, out_bias, first_gain, first_shift, up_weight, up_bias, down_weight, down_bias, second_gain, second_shift):
        queries = low(low_back(product(token_vals, query_weight) + query_bias))
        key_rows = low(low_back(product(token_vals, key_weight)))
        value_rows = low(low_back(product(token_vals, value_weight) + value_bias))
        block_count = token_vals.shape[0] // PACK

        def split_heads(values):
            return values.reshape(block_count, PACK, HEADS, HEAD_DIM)
        mixed, scores = lax.map(jax.checkpoint(attend), (split_heads(queries), split_heads(key_rows), split_heads(value_rows), prev_vals, pair_masks))
        mixed = low(low_back(mixed.reshape(token_vals.shape[0], D)))
        branch = low_back(product(mixed, out_weight) + out_bias)
        normed = layer_norm(token_vals + branch, first_gain, first_shift)
        pre_act = low_back(product(low(normed), up_weight) + up_bias)
        activated = low(jax.nn.gelu(pre_act, approximate=False))
        second = low_back(product(activated, down_weight) + down_bias)
        result = layer_norm(normed + second, second_gain, second_shift)
        return (result, scores)
    params = (query_weight, query_bias, key_weight, value_weight, value_bias, out_weight, out_bias, first_gain, first_shift, up_weight, up_bias, down_weight, down_bias, second_gain, second_shift)
    params = tuple((item.astype(jnp.float32) for item in params))
    (result, scores), backward = jax.vjp(forward, tokens.astype(jnp.float32), prev_logits.astype(jnp.float32), *params)
    grads = backward((out_cotangent.astype(jnp.float32), jnp.zeros_like(scores)))
    return (result.astype(jnp.bfloat16), scores.astype(jnp.bfloat16), grads[0], grads[1].astype(jnp.bfloat16), grads[2], grads[3], grads[4], grads[5], grads[6], grads[7], grads[8], grads[9], grads[10], grads[11], grads[12], grads[13], grads[14], grads[15], grads[16])
```

```python
import functools
import math

import jax
import jax.numpy as jnp
from jax import lax
from jax.experimental import pallas as pl
from jax.experimental.pallas import tpu as pltpu
from jax.sharding import PartitionSpec as P

HEAD_DIM = 64
PACK = 512
UNIT = 128
PAIR = 2 * HEAD_DIM
SLOTS16 = 16

NEGATIVE = -1000000000.0
EPSILON = 1e-05
SCALE = 1.0 / math.sqrt(HEAD_DIM)
BF = jnp.bfloat16
F32 = jnp.float32


def mm(left, right):
    return jnp.dot(left, right, preferred_element_type=F32)


def mm_t(left, right):
    return lax.dot_general(left, right, (((1,), (1,)), ((), ())), preferred_element_type=F32)


def t_mm(left, right):
    return lax.dot_general(left, right, (((0,), (0,)), ((), ())), preferred_element_type=F32)


def shape(dims, dtype=BF):
    return jax.ShapeDtypeStruct(dims, dtype)


def call(body, grid, scalars, ins, outs, scratch=(), aliases=None, vmem=48):
    def spec(block, index):
        if block is None:
            return pl.BlockSpec(memory_space=pl.ANY)
        return pl.BlockSpec(block, index)

    return pl.pallas_call(
        body,
        out_shape=[o[0] for o in outs],
        grid_spec=pltpu.PrefetchScalarGridSpec(
            num_scalar_prefetch=len(scalars),
            grid=grid,
            in_specs=[spec(i[1], i[2]) for i in ins],
            out_specs=[spec(o[1], o[2]) for o in outs],
            scratch_shapes=list(scratch),
        ),
        input_output_aliases=aliases or {},
        compiler_params=pltpu.CompilerParams(vmem_limit_bytes=vmem * 1024 * 1024),
    )(*scalars, *[i[0] for i in ins])


def whole(array):
    dims = array.shape
    return (array, dims, lambda *_: (0,) * len(dims))


def whole_out(dims, dtype=BF):
    return (shape(dims, dtype), dims, lambda *_: (0,) * len(dims))


def fill_bias(scalar_ref, block, bias_ref):
    start = jnp.int32(0)
    rows = lax.broadcasted_iota(jnp.int32, (PACK, 1), 0)
    low = jnp.zeros((PACK, 1), jnp.int32)
    high = jnp.zeros((PACK, 1), jnp.int32)
    for slot in range(4):
        length = scalar_ref[2 + block * 4 + slot]
        finish = start + ((length + (UNIT - 1)) // UNIT) * UNIT
        member = (rows >= start) & (rows < finish)
        low = jnp.where(member, start, low)
        high = jnp.where(member, start + length, high)
        start = finish
    cols = lax.broadcasted_iota(jnp.int32, (PACK, PACK), 1)
    bias_ref[...] = jnp.where((cols >= low) & (cols < high), 0.0, NEGATIVE)


def half_lanes(rows):
    return lax.broadcasted_iota(jnp.int32, (rows, PAIR), 1) < HEAD_DIM


TILE = 128


def attend_body(
    scalar_ref, x_ref, wq_ref, wk_ref, wv_ref, bq_ref, bv_ref, prev_ref,
    q_ref, k_ref, v_ref, mix_ref, lse_ref, bias_ref,
):
    block = scalar_ref[0] + pl.program_id(0)
    pair = pl.program_id(1)

    @pl.when(pair == 0)
    def _():
        fill_bias(scalar_ref, block, bias_ref)
        lse_ref[...] = jnp.zeros_like(lse_ref)

    x = x_ref[...]
    q = (mm(x, wq_ref[...]) + bq_ref[...]).astype(BF)
    k = mm(x, wk_ref[...]).astype(BF)
    v = (mm(x, wv_ref[...]) + bv_ref[...]).astype(BF)
    q_ref[...] = q
    k_ref[...] = k
    v_ref[...] = v
    left = half_lanes(TILE)
    lanes = lax.broadcasted_iota(jnp.int32, (TILE, 128), 1)
    for tile in range(PACK // TILE):
        rows = pl.ds(tile * TILE, TILE)
        mixes = []
        sums = lse_ref[rows, :]
        for head in range(2):
            keep = left if head == 0 else jnp.logical_not(left)
            qh = jnp.where(keep, q_ref[rows, :], 0) * BF(SCALE)
            scores = mm_t(qh, k) + prev_ref[0, head, rows, :].astype(F32)
            masked = scores + bias_ref[rows, :]
            top = jnp.max(masked, axis=-1, keepdims=True)
            powers = jnp.exp(masked - top)
            total = jnp.sum(powers, axis=-1, keepdims=True)
            low = (powers * (1.0 / total)).astype(BF)
            mixes.append(mm(low, v))
            sums = jnp.where(lanes == 2 * pair + head, top + jnp.log(total), sums)
        lse_ref[rows, :] = sums
        mix_ref[rows, :] = jnp.where(left, mixes[0], mixes[1]).astype(BF)


def attend_forward(scalars, tokens, prev, weights, half_rows):
    wq, wk, wv, bq, bv = weights
    blocks = half_rows // PACK
    width = wq.shape[1]
    pairs = width // PAIR
    depth = tokens.shape[1]
    col = lambda i, p, s: (0, p)
    own = lambda i, p, s: (i, p)
    out = (shape((half_rows, width)), (PACK, PAIR), own)
    return call(
        attend_body,
        (blocks, pairs),
        [scalars],
        [
            (tokens, (PACK, depth), lambda i, p, s: (s[0] + i, 0)),
            (wq, (depth, PAIR), col),
            (wk, (depth, PAIR), col),
            (wv, (depth, PAIR), col),
            (bq, (1, PAIR), col),
            (bv, (1, PAIR), col),
            (prev, (1, 2, PACK, PACK), lambda i, p, s: (s[0] + i, p, 0, 0)),
        ],
        [out, out, out, out, (shape((half_rows, 128), F32), (PACK, 128), lambda i, p, s: (i, 0))],
        [pltpu.VMEM((PACK, PACK), F32)],
    )


def attend_back_body(
    scalar_ref, q_ref, k_ref, v_ref, lse_ref, prev_ref, grad_ref, _raw_in, _prev_in,
    raw_ref, pg_ref, dq_ref, dk_ref, dv_ref, bias_ref, low_ref,
):
    block = scalar_ref[0] + pl.program_id(0)
    pair = scalar_ref[1] + pl.program_id(1)

    @pl.when(pl.program_id(1) == 0)
    def _():
        fill_bias(scalar_ref, block, bias_ref)

    k = k_ref[...]
    v = v_ref[...]
    left = half_lanes(TILE)
    lanes = lax.broadcasted_iota(jnp.int32, (TILE, 128), 1)
    for tile in range(PACK // TILE):
        rows = pl.ds(tile * TILE, TILE)
        sides = []
        for head in range(2):
            keep = left if head == 0 else jnp.logical_not(left)
            qh = jnp.where(keep, q_ref[rows, :], 0) * BF(SCALE)
            gh = jnp.where(keep, grad_ref[rows, :], 0)
            lse = jnp.sum(
                jnp.where(lanes == 2 * pair + head, lse_ref[rows, :], 0.0), axis=-1, keepdims=True
            )
            scores = mm_t(qh, k) + prev_ref[0, head, rows, :].astype(F32)
            raw_ref[0, head, rows, :] = scores.astype(BF)
            probs = jnp.exp(scores + bias_ref[rows, :] - lse)
            low_ref[head, rows, :] = probs.astype(BF)
            through = mm_t(gh, v)
            mean = jnp.sum(probs * through, axis=-1, keepdims=True)
            score_low = (probs * (through - mean)).astype(BF)
            pg_ref[0, head, rows, :] = score_low
            sides.append(mm(score_low, k))
        dq_ref[rows, :] = (jnp.where(left, sides[0], sides[1]) * SCALE).astype(BF)
    q = q_ref[...]
    g = grad_ref[...]
    wide = half_lanes(PACK)
    dk = jnp.where(wide, t_mm(pg_ref[0, 0], q), t_mm(pg_ref[0, 1], q))
    dk_ref[...] = (dk * SCALE).astype(BF)
    dv_ref[...] = jnp.where(wide, t_mm(low_ref[0], g), t_mm(low_ref[1], g)).astype(BF)


def attend_backward(scalars, parts, prev, grad, raw, prev_grad, pairs):
    q, k, v, lse = parts
    half_rows = q.shape[0]
    blocks = half_rows // PACK
    own = lambda i, p, s: (i, s[1] + p)
    new = lambda i, p, s: (i, p)
    big = lambda i, p, s: (s[0] + i, s[1] + p, 0, 0)
    block = (PACK, PAIR)
    tall = (1, 2, PACK, PACK)
    out = (shape((half_rows, pairs * PAIR)), block, new)
    if raw is None:
        aliases = {}
        ins = []

        def body(*refs):
            attend_back_body(*refs[:7], None, None, *refs[7:])
    else:
        aliases = {7: 0, 8: 1}
        ins = [(raw, None, None), (prev_grad, None, None)]
        body = attend_back_body
    return call(
        body,
        (blocks, pairs),
        [scalars],
        [
            (q, block, own),
            (k, block, own),
            (v, block, own),
            (lse, (PACK, 128), lambda i, p, s: (i, 0)),
            (prev, tall, big),
            (grad, block, own),
        ]
        + ins,
        [(shape(prev.shape), tall, big), (shape(prev.shape), tall, big), out, out, out],
        [pltpu.VMEM((PACK, PACK), F32), pltpu.VMEM((2, PACK, PACK), BF)],
        aliases,
    )


def norm(values):
    center = values - jnp.mean(values, axis=-1, keepdims=True)
    inverse = lax.rsqrt(jnp.mean(center * center, axis=-1, keepdims=True) + EPSILON)
    return center * inverse, inverse


def norm_back(grad, normal, inverse, gain):
    scaled = grad * gain
    return inverse * (
        scaled
        - jnp.mean(scaled, axis=-1, keepdims=True)
        - normal * jnp.mean(scaled * normal, axis=-1, keepdims=True)
    )


def gelu_parts(z):
    cumulative = 0.5 * (1.0 + lax.erf(z * (1.0 / math.sqrt(2.0))))
    density = jnp.exp(-0.5 * z * z) * (1.0 / math.sqrt(2.0 * math.pi))
    return z * cumulative, cumulative + z * density


ROWS = 32
LN_ROWS = 64


def forward_body(
    scalar_ref, mix_o, mix_s, wo_o, wo_s, tok_ref, ob, g1, s1,
    wu_o, wu_s, bu_o, bu_s, wd_o, wd_s, db, g2, s2, cot_ref,
    act_o, act_s, slope_o, slope_s, normal1, inverse1, normed_t, second_grad, low_ref, low_t,
    out_ref, sums_ref, normed, normed_low, total, pre,
):
    step = pl.program_id(0)
    rows_all = normed.shape[0]

    @pl.when(step == 0)
    def _():
        total[...] = mm(mix_o[...], wo_o[...]) + mm(mix_s[...], wo_s[...])
        for t in range(rows_all // LN_ROWS):
            rows = pl.ds(t * LN_ROWS, LN_ROWS)
            values = tok_ref[rows, :].astype(F32) + (total[rows, :] + ob[...])
            normal, inverse = norm(values)
            normal1[rows, :] = normal
            inverse1[rows, :] = inverse
            result = normal * g1[...] + s1[...]
            normed[rows, :] = result
            normed_low[rows, :] = result.astype(BF)
            total[rows, :] = jnp.zeros_like(result)
        normed_t[...] = normed_low[...].T

    x = normed_low[...]
    for wu, bu, wd, act, slope in (
        (wu_o, bu_o, wd_o, act_o, slope_o),
        (wu_s, bu_s, wd_s, act_s, slope_s),
    ):
        pre[...] = mm(x, wu[...]) + bu[...]

        def tile(t, _):
            rows = pl.ds(pl.multiple_of(t * ROWS, ROWS), ROWS)
            value, grad = gelu_parts(pre[rows, :])
            act[rows, :] = value.astype(BF)
            slope[rows, :] = grad.astype(BF)
            return 0

        lax.fori_loop(0, rows_all // ROWS, tile, 0, unroll=2)
        total[...] += mm(act[...], wd[...])

    @pl.when(step == pl.num_programs(0) - 1)
    def _():
        depth = total.shape[1]
        gain_sum = jnp.zeros((1, depth), F32)
        shift_sum = jnp.zeros((1, depth), F32)
        low_sum = jnp.zeros((1, depth), F32)
        for t in range(rows_all // LN_ROWS):
            rows = pl.ds(t * LN_ROWS, LN_ROWS)
            normal, inverse = norm(normed[rows, :] + (total[rows, :] + db[...]))
            out_ref[rows, :] = (normal * g2[...] + s2[...]).astype(BF)
            grad = cot_ref[rows, :].astype(F32)
            back = norm_back(grad, normal, inverse, g2[...])
            second_grad[rows, :] = back
            low = back.astype(BF)
            low_ref[rows, :] = low
            gain_sum += jnp.sum(grad * normal, axis=0, keepdims=True)
            shift_sum += jnp.sum(grad, axis=0, keepdims=True)
            low_sum += jnp.sum(low.astype(F32), axis=0, keepdims=True)
        low_t[...] = low_ref[...].T
        sums_ref[...] = jnp.concatenate(
            [gain_sum, shift_sum, low_sum, jnp.zeros((5, depth), F32)], axis=0
        )


def ff_forward(scalars, mix_o, mix_s, wo, tokens, ob, g1, s1, wu, bu, wd, db, g2, s2, cot):
    rows, depth = cot.shape
    width = wu[0].shape[1]
    steps = 3
    cut = width // steps
    col = lambda j, s: (0, j)
    row = lambda j, s: (j, 0)
    return call(
        forward_body,
        (steps,),
        [scalars],
        [
            whole(mix_o), whole(mix_s), whole(wo[0]), whole(wo[1]),
            (tokens, (rows, depth), lambda j, s: (s[1], 0)),
            whole(ob), whole(g1), whole(s1),
            (wu[0], (depth, cut), col), (wu[1], (depth, cut), col),
            (bu[0], (1, cut), col), (bu[1], (1, cut), col),
            (wd[0], (cut, depth), row), (wd[1], (cut, depth), row),
            whole(db), whole(g2), whole(s2), whole(cot),
        ],
        [
            (shape((rows, width)), (rows, cut), col),
            (shape((rows, width)), (rows, cut), col),
            (shape((rows, width)), (rows, cut), col),
            (shape((rows, width)), (rows, cut), col),
            whole_out((rows, depth), F32),
            whole_out((rows, 1), F32),
            whole_out((depth, rows)),
            whole_out((rows, depth), F32),
            whole_out((rows, depth)),
            whole_out((depth, rows)),
            whole_out((rows, depth)),
            whole_out((8, depth), F32),
        ],
        [
            pltpu.VMEM((rows, depth), F32),
            pltpu.VMEM((rows, depth), BF),
            pltpu.VMEM((rows, depth), F32),
            pltpu.VMEM((rows, cut), F32),
        ],
    )


def backward_body(
    low, second_grad, wd_o, wd_s, wu_o, wu_s, slope_o, slope_s, normal1, inverse1, g1,
    wo_o, wo_s, mix_o, mix_s,
    pg_o, pg_s, bias_o, bias_s, branch_grad, mg_o, mg_s, wot_o, wot_s, sums_ref,
    total, branch_low,
):
    step = pl.program_id(0)
    rows_all, depth = total.shape

    @pl.when(step == 0)
    def _():
        total[...] = second_grad[...]

    x = low[...]
    for wd, wu, slope, pg, bias in (
        (wd_s, wu_s, slope_s, pg_s, bias_s),
        (wd_o, wu_o, slope_o, pg_o, bias_o),
    ):
        grad = (mm_t(x, wd[...]) * slope[...].astype(F32)).astype(BF)
        pg[...] = grad
        bias[...] = jnp.sum(grad.astype(F32), axis=0, keepdims=True)
        total[...] += mm_t(grad, wu[...])

    @pl.when(step == pl.num_programs(0) - 1)
    def _():
        gain_sum = jnp.zeros((1, depth), F32)
        shift_sum = jnp.zeros((1, depth), F32)
        low_sum = jnp.zeros((1, depth), F32)
        for t in range(rows_all // LN_ROWS):
            rows = pl.ds(t * LN_ROWS, LN_ROWS)
            grad = total[rows, :]
            normal = normal1[rows, :]
            back = norm_back(grad, normal, inverse1[rows, :], g1[...])
            branch_grad[rows, :] = back
            small = back.astype(BF)
            branch_low[rows, :] = small
            gain_sum += jnp.sum(grad * normal, axis=0, keepdims=True)
            shift_sum += jnp.sum(grad, axis=0, keepdims=True)
            low_sum += jnp.sum(small.astype(F32), axis=0, keepdims=True)
        sums_ref[...] = jnp.concatenate(
            [gain_sum, shift_sum, low_sum, jnp.zeros((5, depth), F32)], axis=0
        )
        y = branch_low[...]
        mg_s[...] = mm_t(y, wo_s[...]).astype(BF)
        mg_o[...] = mm_t(y, wo_o[...]).astype(BF)
        turned = y.T
        wot_s[...] = mm(turned, mix_s[...]).astype(BF)
        wot_o[...] = mm(turned, mix_o[...])


def ff_backward(low, second_grad, wd, wu, slopes, normal1, inverse1, g1, wo, mix):
    rows, depth = low.shape
    width = wu[0].shape[1]
    heads = wo[0].shape[0]
    steps = 3
    cut = width // steps
    col = lambda j: (0, j)
    row = lambda j: (j, 0)
    return call(
        backward_body,
        (steps,),
        [],
        [
            whole(low), whole(second_grad),
            (wd[0], (cut, depth), row), (wd[1], (cut, depth), row),
            (wu[0], (depth, cut), col), (wu[1], (depth, cut), col),
            (slopes[0], (rows, cut), col), (slopes[1], (rows, cut), col),
            whole(normal1), whole(inverse1), whole(g1),
            whole(wo[0]), whole(wo[1]), whole(mix[0]), whole(mix[1]),
        ],
        [
            (shape((rows, width)), (rows, cut), col),
            (shape((rows, width)), (rows, cut), col),
            (shape((1, width), F32), (1, cut), col),
            (shape((1, width), F32), (1, cut), col),
            whole_out((rows, depth), F32),
            whole_out((rows, heads)),
            whole_out((rows, heads)),
            whole_out((depth, heads), F32),
            whole_out((depth, heads)),
            whole_out((8, depth), F32),
        ],
        [pltpu.VMEM((rows, depth), F32), pltpu.VMEM((rows, depth), BF)],
    )


def plain_body(left, right, out):
    out[...] = mm(left[...], right[...]).astype(BF)


def product(left, right):
    depth, rows = left.shape
    width = right.shape[1]
    cut = width // 3
    return call(
        plain_body,
        (3,),
        [],
        [whole(left), (right, (rows, cut), lambda j: (0, j))],
        [(shape((depth, width)), (depth, cut), lambda j: (0, j))],
    )[0]


def spread(table_ref, full, send, keep):
    chunk = send.shape[1]
    half = SLOTS16 // 2
    for slot in range(SLOTS16):
        start = pl.multiple_of(table_ref[slot] * chunk, chunk)
        piece = full[pl.ds(start, chunk), :]
        if slot < half:
            keep[slot] = piece
        else:
            send[slot - half] = piece


def group_body(table_ref, left, right, recv, send, keep, full):
    full[...] = (mm(left[...], right[...]) + recv[...].astype(F32)).astype(BF)
    spread(table_ref, full, send, keep)


def group(table, left, right, recv, first, count):
    depth, rows = left.shape
    cut = 384
    half = SLOTS16 // 2
    chunk = depth // SLOTS16
    base = first // cut
    out = (shape((half, chunk, count)), (half, chunk, cut), lambda j, s: (0, 0, j))
    return call(
        group_body,
        (count // cut,),
        [table],
        [
            whole(left),
            (right, (rows, cut), lambda j, s: (0, base + j)),
            (recv, (depth, cut), lambda j, s: (0, base + j)),
        ],
        [out, out],
        [pltpu.VMEM((depth, cut), BF)],
    )


def last_group_body(table_ref, own, recv, lefts, rights, send, keep, full):
    pass


def late_body(with_out, table_ref, *refs):
    if with_out:
        own, recv, tok_a, tok_b, ga, gb, send, keep, full = refs
        full[:, :384] = (own[...] + recv[...].astype(F32)).astype(BF)
        full[:, 384:] = (mm(tok_a[...], ga[...]) + mm(tok_b[...], gb[...])).astype(BF)
    else:
        tok_a, tok_b, ga, gb, ha, hb, send, keep, full = refs
        full[:, :384] = (mm(tok_a[...], ga[...]) + mm(tok_b[...], gb[...])).astype(BF)
        full[:, 384:] = (mm(tok_a[...], ha[...]) + mm(tok_b[...], hb[...])).astype(BF)
    spread(table_ref, full, send, keep)


def late_group(table, with_out, arrays, depth):
    half = SLOTS16 // 2
    chunk = depth // SLOTS16
    count = 2 * 384
    return call(
        functools.partial(late_body, with_out),
        (1,),
        [table],
        [whole(a) for a in arrays],
        [whole_out((half, chunk, count)), whole_out((half, chunk, count))],
        [pltpu.VMEM((depth, count), BF)],
    )


def turn_body(x_ref, y_ref):
    y_ref[...] = x_ref[...].T


def turned_tokens(tokens):
    rows, depth = tokens.shape
    return call(
        turn_body,
        (rows // PACK,),
        [],
        [(tokens, (PACK, depth), lambda i: (i, 0))],
        [(shape((depth, rows)), (depth, PACK), lambda i: (0, i))],
    )[0]


def token_body(dq, dk, dv, wq, wk, wv, out):
    out[...] = (
        mm_t(dq[...], wq[...]) + mm_t(dk[...], wk[...]) + mm_t(dv[...], wv[...])
    ).astype(out.dtype)


def token_part(grads, weights):
    rows = grads[0].shape[0]
    depth = weights[0].shape[0]
    return call(
        token_body,
        (1,),
        [],
        [whole(a) for a in (*grads, *weights)],
        [whole_out((rows, depth))],
    )[0]


def token_sum_body(dq, dk, dv, wq, wk, wv, recv, branch, out):
    out[...] = (
        branch[...]
        + mm_t(dq[...], wq[...])
        + mm_t(dk[...], wk[...])
        + mm_t(dv[...], wv[...])
        + recv[...].astype(F32)
    )


def token_sum(grads, weights, recv, branch):
    rows, depth = branch.shape
    return call(
        token_sum_body,
        (1,),
        [],
        [whole(a) for a in (*grads, *weights, recv, branch)],
        [whole_out((rows, depth), F32)],
    )[0]


def first_add_body(k1, r1, k2, r2, o1, s1, o2, s2):
    for k, r, o, s in ((k1, r1, o1, s1), (k2, r2, o2, s2)):
        half = k.shape[0] // 2
        for part, out in ((0, o), (1, s)):
            rows = pl.ds(part * half, half)
            out[...] = (k[rows].astype(F32) + r[rows].astype(F32)).astype(BF)


def first_add(k1, r1, k2, r2):
    slots, chunk, width = k1.shape
    half = (slots // 2, chunk, width)
    return call(
        first_add_body, (1,), [], [whole(a) for a in (k1, r1, k2, r2)], [whole_out(half)] * 4
    )


def second_add_body(k1, r1, k2, r2, *outs):
    for slot, out in enumerate(outs):
        out[0] = (k1[slot].astype(F32) + r1[slot].astype(F32)).astype(BF)
        out[1] = (k2[slot].astype(F32) + r2[slot].astype(F32)).astype(BF)


def second_add(k1, r1, k2, r2):
    slots, chunk, width = k1.shape
    return call(
        second_add_body,
        (1,),
        [],
        [whole(a) for a in (k1, r1, k2, r2)],
        [whole_out((2, chunk, width))] * slots,
    )


def sum_body(a, b, c, d, out):
    out[...] = (
        (a[...].astype(F32) + b[...].astype(F32)) + (c[...].astype(F32) + d[...].astype(F32))
    ).astype(BF)


def sum_four(a, b, c, d):
    return call(sum_body, (1,), [], [whole(x) for x in (a, b, c, d)], [whole_out(a.shape)])[0]


def stack_body(a, b, c, d, o1, o2):
    for slot, x in enumerate((a, b, c, d)):
        o1[slot] = x[0]
        o2[slot] = x[1]


def stack_four(a, b, c, d):
    _, chunk, width = a.shape
    return call(
        stack_body,
        (1,),
        [],
        [whole(x) for x in (a, b, c, d)],
        [whole_out((4, chunk, width))] * 2,
    )


def join_body(a, b, c, d, o1, o2):
    half = a.shape[0]
    o1[:half] = a[...]
    o1[half:] = b[...]
    o2[:half] = c[...]
    o2[half:] = d[...]


def join(a, b, c, d):
    slots, chunk, width = a.shape
    return call(
        join_body,
        (1,),
        [],
        [whole(x) for x in (a, b, c, d)],
        [whole_out((2 * slots, chunk, width))] * 2,
    )


def gather_rows(table_ref, first, own, recv, full):
    chunk = own.shape[1]
    for half, ref in ((0, own), (8, recv)):
        for slot in range(8):
            start = pl.multiple_of(table_ref[first + half + slot] * chunk, chunk)
            full[pl.ds(start, chunk), :] = ref[slot].astype(full.dtype)


def finish_body(turned, table_ref, a1, b1, a2, b2, out, full):
    step = pl.program_id(0)
    half = pl.num_programs(0) // 2
    target = full if turned else out

    @pl.when(step < half)
    def _():
        gather_rows(table_ref, 0, a1, b1, target)

    @pl.when(step >= half)
    def _():
        gather_rows(table_ref, SLOTS16, a2, b2, target)

    if turned:
        out[...] = full[...].T.astype(F32)


def finish(tables, arrays, turned):
    slots, chunk, width = arrays[0].shape
    depth = 2 * slots * chunk
    cut = 256
    steps = width // cut
    block = (slots, chunk, cut)
    one = lambda j, s: (0, 0, jnp.minimum(j, steps - 1))
    two = lambda j, s: (0, 0, jnp.maximum(j - steps, 0))
    if turned:
        out = (shape((2 * width, depth), F32), (cut, depth), lambda j, s: (j, 0))
    else:
        out = (shape((depth, 2 * width), F32), (depth, cut), lambda j, s: (0, j))
    return call(
        functools.partial(finish_body, turned),
        (2 * steps,),
        [tables],
        [(arrays[0], block, one), (arrays[1], block, one), (arrays[2], block, two), (arrays[3], block, two)],
        [out],
        [pltpu.VMEM((depth, cut), BF)],
    )[0]


def finish_late_body(table_ref, a1, b1, a2, b2, o_ref, q_ref, k_ref, v_ref, full):
    gather_rows(table_ref, 0, a1, b1, full)
    o_ref[...] = full[:, :384].T.astype(F32)
    q_ref[...] = full[:, 384:].astype(F32)
    gather_rows(table_ref, SLOTS16, a2, b2, full)
    k_ref[...] = full[:, :384].astype(F32)
    v_ref[...] = full[:, 384:].astype(F32)


def finish_late(tables, arrays):
    slots, chunk, width = arrays[0].shape
    depth = 2 * slots * chunk
    wide = whole_out((depth, width // 2), F32)
    return call(
        finish_late_body,
        (1,),
        [tables],
        [whole(a) for a in arrays],
        [whole_out((width // 2, depth), F32), wide, wide, wide],
        [pltpu.VMEM((depth, width), BF)],
    )


def swap(value):
    return lax.ppermute(value, "tensor", [(0, 1), (1, 0)])


def across(value, mask):
    size = lax.axis_size("dp")
    return lax.ppermute(value, "dp", [(i, i ^ mask) for i in range(size)])


def extra_masks():
    size = lax.axis_size("dp")
    masks = []
    mask = SLOTS16
    while mask < size:
        masks.append(mask)
        mask *= 2
    return masks


def sum_over_dp(send1, keep1, send2, keep2):
    r1, r2 = across(send1, 1), across(send2, 2)
    o1, s1, o2, s2 = first_add(keep1, r1, keep2, r2)
    r1, r2 = across(s1, 2), across(s2, 1)
    own, *sends = second_add(o1, r1, o2, r2)
    got = [across(s, (m + 1) << 2) for m, s in enumerate(sends)]
    own = sum_four(own, *got)
    for mask in extra_masks():
        own = (own.astype(F32) + across(own, mask).astype(F32)).astype(BF)
    got = [across(own, (m + 1) << 2) for m in range(3)]
    o1, o2 = stack_four(own, *got)
    r1, r2 = across(o1, 2), across(o2, 1)
    o1, o2 = join(o1, r1, o2, r2)
    return o1, across(o1, 1), o2, across(o2, 2)


def tables():
    me = lax.axis_index("dp") % SLOTS16
    slots = jnp.arange(SLOTS16, dtype=jnp.int32)
    high, mid, z = slots // 8, (slots // 4) % 2, slots % 4
    one = high + 2 * mid + 4 * z
    two = 2 * high + mid + 4 * z
    return one ^ me, two ^ me


def on_device(
    tokens, seq_lengths, prev_logits, query_weight, query_bias, key_weight, value_weight,
    value_bias, out_weight, out_bias, first_gain, first_shift, up_weight, up_bias, down_weight,
    down_bias, second_gain, second_shift, out_cotangent,
):
    tok_rows, depth = tokens.shape
    half_rows = tok_rows // 2
    half_blocks = half_rows // PACK
    core = lax.axis_index("tensor")
    lengths = seq_lengths.reshape(-1)
    table1, table2 = tables()
    both = jnp.concatenate([table1, table2])

    def scalars(block, second):
        head = jnp.stack([jnp.int32(block), jnp.int32(second)])
        return jnp.concatenate([head, lengths])

    own_block = core * half_blocks
    sib_block = (1 - core) * half_blocks
    row = lambda v: v.reshape(1, -1)

    wo = (out_weight, swap(out_weight))
    wu = (up_weight, swap(up_weight))
    bu = (row(up_bias), row(swap(up_bias)))
    wd = (down_weight, swap(down_weight))

    qkv = (query_weight, key_weight, value_weight, row(query_bias), row(value_bias))
    *parts_s, mixed_s, lse_s = attend_forward(
        scalars(sib_block, 0), tokens, prev_logits, qkv, half_rows
    )
    mixed_r = swap(mixed_s)
    *parts_o, mixed_o, lse_o = attend_forward(
        scalars(own_block, 0), tokens, prev_logits, qkv, half_rows
    )
    (
        act_o, act_s, slope_o, slope_s, normal1, inverse1, normed_t, second_grad, second_low,
        second_low_t, layer_output, sums2,
    ) = ff_forward(
        scalars(0, core), mixed_o, mixed_r, wo, tokens, row(out_bias), row(first_gain),
        row(first_shift), wu, bu, wd, row(down_bias), row(second_gain), row(second_shift),
        out_cotangent,
    )
    down_r = swap(product(second_low_t, act_s))
    (
        pg_o, pg_s, ubias_o, ubias_s, branch_grad, mg_o, mg_s, wot_o, wot_s, sums1,
    ) = ff_backward(
        second_low, second_grad, wd, wu, (slope_o, slope_s), normal1, inverse1, row(first_gain),
        wo, (mixed_o, mixed_r),
    )
    mg_r = swap(mg_s)
    width = depth
    down = sum_over_dp(
        *group(table1, second_low_t, act_o, down_r, 0, width),
        *group(table2, second_low_t, act_o, down_r, width, width),
    )
    up_r = swap(product(normed_t, pg_s))
    wot_r = swap(wot_s)
    up = sum_over_dp(
        *group(table1, normed_t, pg_o, up_r, 0, width),
        *group(table2, normed_t, pg_o, up_r, width, width),
    )
    down_weight_grad = finish(both, down, True)
    up_weight_grad = finish(both, up, False)

    pairs = query_weight.shape[1] // PAIR
    raw, prev_grad, *grads_o = attend_backward(
        scalars(own_block, 0), (*parts_o, lse_o), prev_logits, mg_o, None, None, pairs
    )
    raw, prev_grad, *grads_s = attend_backward(
        scalars(sib_block, 0), (*parts_s, lse_s), prev_logits, mg_r, raw, prev_grad, pairs
    )
    tokens_t = turned_tokens(tokens)
    tok_o = lax.dynamic_slice_in_dim(tokens_t, core * half_rows, half_rows, 1)
    tok_s = lax.dynamic_slice_in_dim(tokens_t, (1 - core) * half_rows, half_rows, 1)
    late = sum_over_dp(
        *late_group(table1, True, (wot_o, wot_r, tok_o, tok_s, grads_o[0], grads_s[0]), depth),
        *late_group(
            table2, False, (tok_o, tok_s, grads_o[1], grads_s[1], grads_o[2], grads_s[2]), depth
        ),
    )
    out_weight_grad, query_weight_grad, key_weight_grad, value_weight_grad = finish_late(both, late)

    weights = (query_weight, key_weight, value_weight)
    token_r = swap(token_part(grads_s, weights))
    token_grad = token_sum(grads_o, weights, token_r, branch_grad)

    query_sum = jnp.sum(grads_o[0], axis=0, dtype=F32) + jnp.sum(grads_s[0], axis=0, dtype=F32)
    value_sum = jnp.sum(grads_o[2], axis=0, dtype=F32) + jnp.sum(grads_s[2], axis=0, dtype=F32)
    shared = jnp.concatenate([sums2[:3].reshape(-1), sums1[:3].reshape(-1), ubias_o[0]])
    other = swap(jnp.concatenate([sums2[:3].reshape(-1), sums1[:3].reshape(-1), ubias_s[0]]))
    small = jnp.concatenate([shared + other, query_sum, value_sum]).reshape(-1, 128)
    mask = 1
    while mask < lax.axis_size("dp"):
        small = small + across(small, mask)
        mask *= 2
    small = small.reshape(-1)
    cuts = []
    start = 0
    for count in (depth,) * 6 + (ubias_o.shape[1], query_sum.shape[0], value_sum.shape[0]):
        cuts.append(small[start : start + count])
        start += count
    (
        second_gain_grad, second_shift_grad, down_bias_grad, first_gain_grad, first_shift_grad,
        out_bias_grad, up_bias_grad, query_bias_grad, value_bias_grad,
    ) = cuts
    return (
        layer_output, raw, token_grad, prev_grad,
        query_weight_grad, query_bias_grad, key_weight_grad, value_weight_grad, value_bias_grad,
        out_weight_grad, out_bias_grad, first_gain_grad, first_shift_grad,
        up_weight_grad, up_bias_grad, down_weight_grad, down_bias_grad,
        second_gain_grad, second_shift_grad,
    )


def solution(mesh):
    return jax.shard_map(
        on_device,
        mesh=mesh,
        in_specs=(
            P("dp", None),
            P("dp", None),
            P("dp", "tensor", None, None),
            P(None, "tensor"),
            P("tensor"),
            P(None, "tensor"),
            P(None, "tensor"),
            P("tensor"),
            P("tensor", None),
            P(),
            P(),
            P(),
            P(None, "tensor"),
            P("tensor"),
            P("tensor", None),
            P(),
            P(),
            P(),
            P(("dp", "tensor"), None),
        ),
        out_specs=(
            P(("dp", "tensor"), None),
            P("dp", "tensor", None, None),
            P(("dp", "tensor"), None),
            P("dp", "tensor", None, None),
            P(None, "tensor"),
            P("tensor"),
            P(None, "tensor"),
            P(None, "tensor"),
            P("tensor"),
            P("tensor", None),
            P(),
            P(),
            P(),
            P(None, "tensor"),
            P("tensor"),
            P("tensor", None),
            P(),
            P(),
            P(),
        ),
        check_vma=False,
    )
```
